512 devices in a mesh: group: 8 (over z_lo, core), seq: 64 (over y, x, z_hi).
Axes of the slice: x: 4, y: 4, z: 16 (z_hi: 4, z_lo: 4; z = z_hi * 4 + z_lo), core: 2. Of those that a mesh axis runs over, the one named last changes fastest.
Arguments:
- resp_queries: bfloat16 [8, 8192, 2048], P('group', 'seq'), may hold values from -30 to 30
- resp_keys: bfloat16 [8, 8192, 1024], P('group', 'seq'), may hold values from -6 to 6
- resp_values: bfloat16 [8, 8192, 1024], P('group', 'seq'), may hold values from -6 to 6
- grad_out: bfloat16 [8, 8192, 2048], P('group', 'seq'), may hold values from -6 to 6
- prompt_keys: bfloat16 [8, 128, 1024], P('group', 'seq'), may hold values from -6 to 6
- prompt_values: bfloat16 [8, 128, 1024], P('group', 'seq'), may hold values from -6 to 6
- rewards: float32 [8, 16], P('group'), may hold values from -4 to 4
- lengths: int32 [8, 16], P('group'), may hold values from 1 to 512, as said below
Outputs:
- query_grad: bfloat16 [8, 8192, 2048], P('group', 'seq')
- key_grad: bfloat16 [8, 8192, 1024], P('group', 'seq')
- value_grad: bfloat16 [8, 8192, 1024], P('group', 'seq')
- prompt_key_grad: bfloat16 [8, 128, 1024], P('group', 'seq')
- prompt_value_grad: bfloat16 [8, 128, 1024], P('group', 'seq')
The draws below stay inside these ranges and needn't reach their ends.
Inputs may be any that keep to these rules, and one draw needn't show every extreme that they name: `lengths`: in every prompt one response has exactly 512 tokens.
All inputs are finite; a program needn't handle non-finite values.
Results may differ from the reference program's by a relative error of at most 0.022.
Values may be sent and summed in bfloat16 or wider, within the bound.
No kernel may reach another device: no remote copies, remote signals or barrier semaphores. Data moves between devices by JAX's collectives and lax.ppermute only.
A program may use at most 64 MiB of HBM per device.

```python
import jax
import jax.numpy as jnp
from jax import lax

HEADS = 16
KV_HEADS = 8
HEAD_DIM = 128
RESP_MAX = 512
NRESP = 16
PROMPT = 128
RESP_ALL = 8192
GROUPS = 8


def draw_lengths(key, part):
    key = jax.random.fold_in(key, 11)
    key_len, key_long = jax.random.split(key)
    group_ids = jnp.arange(GROUPS, dtype=jnp.int32)
    lowest = jnp.maximum(1, RESP_MAX * group_ids // GROUPS)
    spread_count = RESP_MAX - lowest + 1
    raw_bits = jax.random.randint(key_len, (GROUPS, NRESP), 0, 1 << 30, dtype=jnp.int32)
    drawn = lowest[:, None] + raw_bits % spread_count[:, None]
    longest = jax.random.randint(key_long, (GROUPS,), 0, NRESP, dtype=jnp.int32)
    slots = jnp.arange(NRESP, dtype=jnp.int32)
    drawn = jnp.where(slots[None, :] == longest[:, None], RESP_MAX, drawn)
    return jnp.minimum(drawn, RESP_MAX).astype(jnp.int32)


def steps_of(rng, shape, shards, low, high):
    level, own = 1.0, jax.random.fold_in(rng, 6)
    for position, blocks in shards:
        draws = jnp.exp(jax.random.uniform(jax.random.fold_in(own, position), (blocks,), jnp.float32, low / len(shards), high / len(shards)))
        level = level * jnp.repeat(draws, shape[position] // blocks).reshape([-1 if axis == position else 1 for axis in range(len(shape))])
    return level


def scatter_about(rng, extent, scale, bound, cuts=(), held_as=jnp.bfloat16):
    values = jax.random.normal(rng, extent, jnp.float32) * scale
    if len(cuts) > 0:
        values = steps_of(rng, extent, cuts, -0.22, 0.18) * values
    return jnp.clip(values, min=-bound, max=bound).astype(held_as)


def setup_inputs(seed: int = 0) -> dict:
    arg_keys = jax.random.split(jax.random.key(seed), 9)
    resp_queries = scatter_about(arg_keys[0], (GROUPS, RESP_ALL, HEADS * HEAD_DIM), 5.0, 30.0, ((0, 8), (1, 64)))
    resp_keys = scatter_about(arg_keys[1], (GROUPS, RESP_ALL, KV_HEADS * HEAD_DIM), 1.0, 6.0, ((0, 8), (1, 64)))
    resp_values = scatter_about(arg_keys[2], (GROUPS, RESP_ALL, KV_HEADS * HEAD_DIM), 1.0, 6.0, ((0, 8), (1, 64)))
    grad_out = scatter_about(arg_keys[3], (GROUPS, RESP_ALL, HEADS * HEAD_DIM), 1.0, 6.0, ((0, 8), (1, 64)))
    prompt_keys = scatter_about(arg_keys[4], (GROUPS, PROMPT, KV_HEADS * HEAD_DIM), 1.0, 6.0, ((0, 8), (1, 64)))
    prompt_values = scatter_about(arg_keys[5], (GROUPS, PROMPT, KV_HEADS * HEAD_DIM), 1.0, 6.0, ((0, 8), (1, 64)))
    rewards = scatter_about(arg_keys[6], (GROUPS, NRESP), 1.0, 4.0, ((0, 8),), jnp.float32)
    lengths = draw_lengths(jax.random.fold_in(arg_keys[8], 71), 0)
    return {"resp_queries": resp_queries, "resp_keys": resp_keys, "resp_values": resp_values, "grad_out": grad_out, "prompt_keys": prompt_keys, "prompt_values": prompt_values, "rewards": rewards, "lengths": lengths}


score_scale = 144.0 ** -0.5
logit_cap = 50.0


def attend(queries, key_rows, value_rows, grad_rows, key_pos, query_pos):
    query_f = queries.astype(jnp.float32)
    key_f = key_rows.astype(jnp.float32)
    value_f = value_rows.astype(jnp.float32)
    raw_score = jnp.einsum("qgjd,kgd->qgjk", query_f, key_f) * score_scale
    capped = logit_cap * jnp.tanh(raw_score / logit_cap)
    visible = (key_pos[None, :] <= query_pos[:, None]) & (key_pos[None, :] >= 0)
    visible = visible[:, None, None, :]
    exp_score = jnp.where(visible, jnp.exp(capped), jnp.float32(0.0))
    attn_weight = exp_score / jnp.sum(exp_score, axis=-1, keepdims=True)
    weight_low = attn_weight.astype(jnp.bfloat16)
    output = jnp.einsum("qgjk,kgd->qgjd", weight_low.astype(jnp.float32), value_f).astype(jnp.bfloat16)
    grad_f = grad_rows.astype(jnp.float32)
    row_delta = jnp.sum(grad_f * output.astype(jnp.float32), axis=-1, keepdims=True)
    grad_weight = jnp.einsum("qgjd,kgd->qgjk", grad_f, value_f)
    grad_score = (attn_weight * (grad_weight - row_delta) * (1.0 - (capped / logit_cap) ** 2) * score_scale).astype(jnp.bfloat16)
    score_f = grad_score.astype(jnp.float32)
    grad_query = jnp.einsum("qgjk,kgd->qgjd", score_f, key_f)
    grad_key = jnp.einsum("qgjk,qgjd->kgd", score_f, query_f)
    grad_value = jnp.einsum("qgjk,qgjd->kgd", weight_low.astype(jnp.float32), grad_f)
    return grad_query, grad_key, grad_value


def reference(resp_queries, resp_keys, resp_values, grad_out, prompt_keys, prompt_values, rewards, lengths):
    count = jnp.sum(lengths.astype(jnp.float32))
    advantage = rewards - jnp.mean(rewards, axis=1, keepdims=True)
    weight = advantage * jnp.float32(GROUPS * NRESP * RESP_MAX) / count
    positions = jnp.arange(RESP_MAX, dtype=jnp.int32)
    key_pos = jnp.concatenate([jnp.zeros((PROMPT,), jnp.int32), positions])
    pair = HEADS // KV_HEADS
    query_outs, key_outs, value_outs, pkey_outs, pvalue_outs = [], [], [], [], []
    for group_id in range(GROUPS):
        prompt_k = prompt_keys[group_id].reshape(PROMPT, KV_HEADS, HEAD_DIM)
        prompt_v = prompt_values[group_id].reshape(PROMPT, KV_HEADS, HEAD_DIM)

        def one_response(response_item):
            queries, key_rows, value_rows, upstream, resp_weight, resp_length = response_item
            live = positions < resp_length
            scaled = jnp.where(live, resp_weight, jnp.float32(0.0))[:, None] * upstream.astype(jnp.float32)
            grad_rows = scaled.astype(jnp.bfloat16).reshape(RESP_MAX, KV_HEADS, pair, HEAD_DIM)
            all_keys = jnp.concatenate([prompt_k, key_rows.reshape(RESP_MAX, KV_HEADS, HEAD_DIM)], axis=0)
            all_values = jnp.concatenate([prompt_v, value_rows.reshape(RESP_MAX, KV_HEADS, HEAD_DIM)], axis=0)
            grad_query, grad_key, grad_value = attend(queries.reshape(RESP_MAX, KV_HEADS, pair, HEAD_DIM), all_keys, all_values, grad_rows, key_pos, positions)
            return (grad_query.reshape(RESP_MAX, HEADS * HEAD_DIM).astype(jnp.bfloat16),
                    grad_key[PROMPT:].reshape(RESP_MAX, KV_HEADS * HEAD_DIM).astype(jnp.bfloat16),
                    grad_value[PROMPT:].reshape(RESP_MAX, KV_HEADS * HEAD_DIM).astype(jnp.bfloat16),
                    grad_key[:PROMPT].reshape(PROMPT, KV_HEADS * HEAD_DIM),
                    grad_value[:PROMPT].reshape(PROMPT, KV_HEADS * HEAD_DIM))

        results = lax.map(one_response, (
            resp_queries[group_id].reshape(NRESP, RESP_MAX, HEADS * HEAD_DIM),
            resp_keys[group_id].reshape(NRESP, RESP_MAX, KV_HEADS * HEAD_DIM),
            resp_values[group_id].reshape(NRESP, RESP_MAX, KV_HEADS * HEAD_DIM),
            grad_out[group_id].reshape(NRESP, RESP_MAX, HEADS * HEAD_DIM),
            weight[group_id], lengths[group_id]))
        query_outs.append(results[0].reshape(RESP_ALL, HEADS * HEAD_DIM))
        key_outs.append(results[1].reshape(RESP_ALL, KV_HEADS * HEAD_DIM))
        value_outs.append(results[2].reshape(RESP_ALL, KV_HEADS * HEAD_DIM))
        pkey_outs.append(jnp.sum(results[3], axis=0).astype(jnp.bfloat16))
        pvalue_outs.append(jnp.sum(results[4], axis=0).astype(jnp.bfloat16))
    return (jnp.stack(query_outs), jnp.stack(key_outs), jnp.stack(value_outs), jnp.stack(pkey_outs), jnp.stack(pvalue_outs))
```

```python
import jax
import jax.numpy as jnp
from jax import lax
from jax.experimental import pallas as pl
from jax.experimental.pallas import tpu as pltpu
from jax.sharding import PartitionSpec as P

HEAD_DIM = 128
RESP_DEVS = 4
RESP_MAX = 512
CHUNKS = 2

SCORE_SCALE = 144.0 ** (-0.5)
LOGIT_CAP = 50.0
VMEM_BYTES = 48 * 1024 * 1024


def contract(left, right, left_dim, right_dim):
    return lax.dot_general(
        left, right, (((left_dim,), (right_dim,)), ((), ())), preferred_element_type=jnp.float32
    )


def pack_kernel(key_ref, value_ref, *packed):
    width = packed[0].shape[1] // 2
    for chunk, out in enumerate(packed):
        cols = slice(chunk * width, (chunk + 1) * width)
        out[:, :width] = key_ref[0, :, cols]
        out[:, width:] = value_ref[0, :, cols]


def pack(keys, values):
    _, rows, width = keys.shape
    out = jax.ShapeDtypeStruct((rows, 2 * width // CHUNKS), keys.dtype)
    return pl.pallas_call(
        pack_kernel,
        out_shape=[out] * CHUNKS,
        compiler_params=pltpu.CompilerParams(vmem_limit_bytes=VMEM_BYTES),
        name="pack",
    )(keys, values)


def attend_kernel(
    place_ref, weight_ref, query_ref, grad_ref, prompt_ref, own_ref, *rest
):
    far_refs = rest[: RESP_DEVS - 1]
    dquery_ref, dprompt_ref, down_ref = rest[RESP_DEVS - 1 : RESP_DEVS + 2]
    dfar_refs = rest[RESP_DEVS + 2 :]
    rows = own_ref.shape[0]
    width = own_ref.shape[1] // 2
    place, length = place_ref[0], place_ref[1]
    weight = weight_ref[0]
    pair = query_ref.shape[2] // width
    slot = place * rows + lax.broadcasted_iota(jnp.int32, (rows, 1), 0)
    row_weight = jnp.where(slot < length, weight, jnp.float32(0.0))
    prompt_rows = prompt_ref.shape[0]
    total_keys = prompt_rows + RESP_DEVS * rows
    key_index = lax.broadcasted_iota(jnp.int32, (pair * rows, total_keys), 1)
    row_index = lax.broadcasted_iota(jnp.int32, (pair * rows, total_keys), 0) % rows
    last_far = prompt_rows + rows * (1 + place)
    own_key = key_index - prompt_rows
    visible = (key_index < last_far) & ((own_key >= rows) | (own_key <= row_index))
    blocks = [prompt_ref, own_ref, *far_refs]
    for head in range(width // HEAD_DIM):
        kcols = slice(head * HEAD_DIM, (head + 1) * HEAD_DIM)
        vcols = slice(width + head * HEAD_DIM, width + (head + 1) * HEAD_DIM)
        keys = jnp.concatenate([block[:, kcols] for block in blocks], axis=0)
        values = jnp.concatenate([block[:, vcols] for block in blocks], axis=0)
        qcols = [
            slice((head * pair + i) * HEAD_DIM, (head * pair + i + 1) * HEAD_DIM)
            for i in range(pair)
        ]
        queries = jnp.concatenate([query_ref[0, :, cols] for cols in qcols], axis=0)
        grads = jnp.concatenate(
            [
                (row_weight * grad_ref[0, :, cols].astype(jnp.float32)).astype(jnp.bfloat16)
                for cols in qcols
            ],
            axis=0,
        )
        squashed = jnp.tanh(contract(queries, keys, 1, 1) * (SCORE_SCALE / LOGIT_CAP))
        exp_score = jnp.where(visible, jnp.exp(LOGIT_CAP * squashed), jnp.float32(0.0))
        attn = exp_score * (1.0 / jnp.sum(exp_score, axis=1, keepdims=True))
        attn_low = attn.astype(jnp.bfloat16)
        output = contract(attn_low, values, 1, 0).astype(jnp.bfloat16)
        delta = jnp.sum(
            grads.astype(jnp.float32) * output.astype(jnp.float32), axis=1, keepdims=True
        )
        grad_weight = contract(grads, values, 1, 1)
        grad_score = (
            attn * (grad_weight - delta) * (SCORE_SCALE - SCORE_SCALE * squashed * squashed)
        ).astype(jnp.bfloat16)
        dquery = contract(grad_score, keys, 1, 0).astype(jnp.bfloat16)
        for i, cols in enumerate(qcols):
            dquery_ref[:, cols] = dquery[i * rows : (i + 1) * rows]
        dkeys = contract(grad_score, queries, 0, 0)
        dvalues = contract(attn_low, grads, 0, 0)
        start = 0
        for out in (dprompt_ref, down_ref, *dfar_refs):
            stop = start + out.shape[0]
            out[:, kcols] = dkeys[start:stop].astype(out.dtype)
            out[:, vcols] = dvalues[start:stop].astype(out.dtype)
            start = stop


def attend_chunk(chunk, place, weight, queries, grads, prompt, own, far):
    rows, both = own.shape
    qwidth = queries.shape[2] // CHUNKS
    whole = lambda array: pl.BlockSpec(array.shape, lambda i: (0,) * array.ndim)
    column = pl.BlockSpec((1, rows, qwidth), lambda i: (0, 0, chunk))
    smem = pl.BlockSpec(memory_space=pltpu.SMEM)
    outs = [
        jax.ShapeDtypeStruct((rows, qwidth), jnp.bfloat16),
        jax.ShapeDtypeStruct(prompt.shape, jnp.bfloat16),
        jax.ShapeDtypeStruct(own.shape, jnp.float32),
    ] + [jax.ShapeDtypeStruct(own.shape, jnp.bfloat16) for _ in far]
    keys = prompt.shape[0] + RESP_DEVS * rows
    return pl.pallas_call(
        attend_kernel,
        grid=(1,),
        in_specs=[smem, smem, column, column, whole(prompt), whole(own)] + [whole(f) for f in far],
        out_specs=[whole(o) for o in outs],
        out_shape=outs,
        compiler_params=pltpu.CompilerParams(vmem_limit_bytes=VMEM_BYTES),
        cost_estimate=pl.CostEstimate(
            flops=0,
            bytes_accessed=0,
            transcendentals=0,
        ),
        name="attend",
    )(place, weight, queries, grads, prompt, own, *far)


def spread(value, axis, groups=None):
    size = len(groups[0]) if groups else lax.axis_size(axis)
    copies = jnp.broadcast_to(value[None], (size, *value.shape))
    return lax.all_to_all(copies, axis, 0, 0, axis_index_groups=groups)


def body(
    resp_queries, resp_keys, resp_values, grad_out, prompt_keys, prompt_values, rewards, lengths
):
    block_rows = resp_queries.shape[1]
    kv_width = resp_keys.shape[2]
    half = kv_width // CHUNKS
    seq_size = lax.axis_size("seq")
    resp_all = seq_size // RESP_DEVS
    seq_index = lax.axis_index("seq")
    place = seq_index % RESP_DEVS
    response_id = seq_index // RESP_DEVS
    resp_count = lengths.shape[1]
    along = [[r * RESP_DEVS + b for b in range(RESP_DEVS)] for r in range(resp_all)]
    across = [[r * RESP_DEVS + b for r in range(resp_all)] for b in range(RESP_DEVS)]

    def shifted(value, by):
        pairs = [
            (line[b], line[b + by])
            for line in along
            for b in range(RESP_DEVS)
            if 0 <= b + by < RESP_DEVS
        ]
        return lax.ppermute(value, "seq", pairs)

    own = pack(resp_keys, resp_values)
    far = [[shifted(own[c], d) for d in range(1, RESP_DEVS)] for c in range(CHUNKS)]

    prompt_own = jnp.concatenate([prompt_keys[0], prompt_values[0]], axis=1)
    rows_here = prompt_own.shape[0]
    prompt_line = spread(prompt_own, "seq", along).reshape(RESP_DEVS * rows_here, 2 * kv_width)
    prompt = spread(prompt_line, "seq", across).reshape(seq_size * rows_here, 2 * kv_width)

    group_count = jnp.sum(lengths.astype(jnp.float32)).reshape(1, 1)
    count = jnp.sum(spread(group_count, "group"))
    advantage = rewards[0] - jnp.mean(rewards[0])
    weight_all = advantage * jnp.float32(lax.axis_size("group") * resp_count * RESP_MAX) / count
    chosen = jnp.arange(resp_count, dtype=jnp.int32) == response_id
    weight = jnp.sum(jnp.where(chosen, weight_all, jnp.float32(0.0))).reshape(1)
    length = jnp.sum(jnp.where(chosen, lengths[0], 0))
    where_it_is = jnp.stack([place, length]).astype(jnp.int32)

    dquery, dprompt, down, back = [], [], [], []
    for c in range(CHUNKS):
        cols = slice(c * half, (c + 1) * half)
        prompt_chunk = jnp.concatenate(
            [prompt[:, cols], prompt[:, kv_width + c * half : kv_width + (c + 1) * half]], axis=1
        )
        outs = attend_chunk(
            c, where_it_is, weight, resp_queries, grad_out, prompt_chunk, own[c], far[c]
        )
        dquery.append(outs[0])
        dprompt.append(outs[1])
        down.append(outs[2])
        back.append([shifted(outs[2 + d], -d) for d in range(1, RESP_DEVS)])

    terms = jnp.concatenate(
        [t[:, :half] for t in dprompt] + [t[:, half:] for t in dprompt], axis=1
    )
    sent = terms.reshape(resp_all, RESP_DEVS * rows_here, 2 * kv_width)
    got = lax.all_to_all(sent, "seq", 0, 0, axis_index_groups=across)
    line_sum = jnp.sum(got.astype(jnp.float32), axis=0).astype(jnp.bfloat16)
    got = lax.all_to_all(
        line_sum.reshape(RESP_DEVS, rows_here, 2 * kv_width), "seq", 0, 0, axis_index_groups=along
    )
    prompt_sum = jnp.sum(got.astype(jnp.float32), axis=0).astype(jnp.bfloat16)

    total = [
        down[c] + sum(b.astype(jnp.float32) for b in back[c]) for c in range(CHUNKS)
    ]
    dkey = jnp.concatenate([t[:, :half].astype(jnp.bfloat16) for t in total], axis=1)
    dvalue = jnp.concatenate([t[:, half:].astype(jnp.bfloat16) for t in total], axis=1)
    return (
        jnp.concatenate(dquery, axis=1)[None],
        dkey[None],
        dvalue[None],
        prompt_sum[None, :, :kv_width],
        prompt_sum[None, :, kv_width:],
    )


def solution(mesh):
    split = P("group", "seq", None)
    return jax.shard_map(
        body,
        mesh=mesh,
        in_specs=(split,) * 6 + (P("group", None),) * 2,
        out_specs=(split,) * 5,
        check_vma=False,
    )
```

```python
import jax
import jax.numpy as jnp
from jax import lax
from jax.experimental import pallas as pl
from jax.experimental.pallas import tpu as pltpu
from jax.sharding import PartitionSpec as P

HEAD_DIM = 128
RESP_DEVS = 4
RESP_MAX = 512
LOW_HEADS = 5

SCORE_SCALE = 144.0 ** (-0.5)
LOGIT_CAP = 50.0
VMEM_BYTES = 48 * 1024 * 1024
PARAMS = dict(compiler_params=pltpu.CompilerParams(vmem_limit_bytes=VMEM_BYTES))


def contract(left, right, left_dim, right_dim):
    return lax.dot_general(
        left, right, (((left_dim,), (right_dim,)), ((), ())), preferred_element_type=jnp.float32
    )


def pack_kernel(key_ref, value_ref, all_ref, low_ref, high_ref):
    low = low_ref.shape[2]
    for part, ref in enumerate((key_ref, value_ref)):
        all_ref[part] = ref[0]
        low_ref[part] = ref[0, :, :low]
        high_ref[part] = ref[0, :, low:]


def pack(keys, values):
    _, rows, width = keys.shape
    low = LOW_HEADS * HEAD_DIM
    return pl.pallas_call(
        pack_kernel,
        out_shape=[
            jax.ShapeDtypeStruct((2, rows, wide), keys.dtype) for wide in (width, low, width - low)
        ],
        name="pack",
        **PARAMS,
    )(keys, values)


def attend_kernel(place_ref, weight_ref, query_ref, grad_ref, prompt_key_ref, prompt_value_ref, own_ref, *rest):
    fars = rest[: RESP_DEVS - 1]
    dquery_ref, dprompt_key_ref, dprompt_value_ref, down_ref, *dfars = rest[-(RESP_DEVS + 3) :]
    rows = query_ref.shape[1]
    pair = query_ref.shape[2] // HEAD_DIM
    place, length = place_ref[0], place_ref[1]
    slot = place * rows + lax.broadcasted_iota(jnp.int32, (rows, 1), 0)
    row_weight = jnp.where(slot < length, weight_ref[0], jnp.float32(0.0))
    blocks = [own_ref, *fars]
    prompt_rows = prompt_key_ref.shape[0]
    total_keys = prompt_rows + RESP_DEVS * rows
    key_index = lax.broadcasted_iota(jnp.int32, (pair * rows, total_keys), 1)
    row_index = lax.broadcasted_iota(jnp.int32, (pair * rows, total_keys), 0) % rows
    last_far = prompt_rows + rows * (1 + place)
    own_key = key_index - prompt_rows
    visible = (key_index < last_far) & ((own_key >= rows) | (own_key <= row_index))
    keys = jnp.concatenate([prompt_key_ref[...]] + [block[0] for block in blocks], axis=0)
    values = jnp.concatenate([prompt_value_ref[...]] + [block[1] for block in blocks], axis=0)
    cols = [slice(i * HEAD_DIM, (i + 1) * HEAD_DIM) for i in range(pair)]
    queries = jnp.concatenate([query_ref[0, :, c] for c in cols], axis=0)
    grads = jnp.concatenate(
        [(row_weight * grad_ref[0, :, c].astype(jnp.float32)).astype(jnp.bfloat16) for c in cols],
        axis=0,
    )
    squashed = jnp.tanh(contract(queries, keys, 1, 1) * (SCORE_SCALE / LOGIT_CAP))
    exp_score = jnp.where(visible, jnp.exp(LOGIT_CAP * squashed), jnp.float32(0.0))
    attn = exp_score * (1.0 / jnp.sum(exp_score, axis=1, keepdims=True))
    attn_low = attn.astype(jnp.bfloat16)
    output = contract(attn_low, values, 1, 0).astype(jnp.bfloat16)
    delta = jnp.sum(grads.astype(jnp.float32) * output.astype(jnp.float32), axis=1, keepdims=True)
    grad_weight = contract(grads, values, 1, 1)
    grad_score = (
        attn * (grad_weight - delta) * (SCORE_SCALE - SCORE_SCALE * squashed * squashed)
    ).astype(jnp.bfloat16)
    dquery = contract(grad_score, keys, 1, 0).astype(jnp.bfloat16)
    for i, c in enumerate(cols):
        dquery_ref[0, :, c] = dquery[i * rows : (i + 1) * rows]
    dkeys = contract(grad_score, queries, 0, 0)
    dvalues = contract(attn_low, grads, 0, 0)
    dprompt_key_ref[...] = dkeys[:prompt_rows].astype(dprompt_key_ref.dtype)
    dprompt_value_ref[...] = dvalues[:prompt_rows].astype(dprompt_value_ref.dtype)
    start = prompt_rows
    for out in (down_ref, *dfars):
        stop = start + out.shape[1]
        out[0] = dkeys[start:stop].astype(out.dtype)
        out[1] = dvalues[start:stop].astype(out.dtype)
        start = stop


def attend_chunk(first, heads, where_it_is, weight, queries, grads, prompt, own, far, so_far):
    rows = queries.shape[1]
    all_heads = prompt.shape[1] // 2 // HEAD_DIM
    width = heads * HEAD_DIM
    qcols = queries.shape[2] // all_heads
    smem = pl.BlockSpec(memory_space=pltpu.SMEM)
    query_spec = pl.BlockSpec((1, rows, qcols), lambda i: (0, 0, first + i))
    prompt_block = (prompt.shape[0], HEAD_DIM)
    key_spec = pl.BlockSpec(prompt_block, lambda i: (0, first + i))
    value_spec = pl.BlockSpec(prompt_block, lambda i: (0, all_heads + first + i))
    own_spec = pl.BlockSpec((2, rows, HEAD_DIM), lambda i: (0, 0, i))
    held_specs = [
        pl.BlockSpec(
            (2, rows, HEAD_DIM),
            lambda i, base=first if held.shape[2] > width else 0: (0, 0, base + i),
        )
        for held in (own, *far)
    ]
    outs = [
        jax.ShapeDtypeStruct(queries.shape, jnp.bfloat16),
        jax.ShapeDtypeStruct((prompt.shape[0], all_heads * HEAD_DIM), jnp.bfloat16),
        jax.ShapeDtypeStruct((prompt.shape[0], all_heads * HEAD_DIM), jnp.bfloat16),
        jax.ShapeDtypeStruct((2, rows, width), jnp.float32),
    ] + [jax.ShapeDtypeStruct((2, rows, width), jnp.bfloat16) for _ in far]
    inputs = [where_it_is, weight, queries, grads, prompt, prompt, own, *far]
    specs = [smem, smem, query_spec, query_spec, key_spec, value_spec] + held_specs
    aliases = {len(inputs) + i: i for i in range(len(so_far))}
    return pl.pallas_call(
        attend_kernel,
        grid=(heads,),
        in_specs=specs + [pl.BlockSpec(memory_space=pl.ANY)] * len(so_far),
        out_specs=[query_spec, key_spec, key_spec] + [own_spec] * RESP_DEVS,
        out_shape=outs,
        input_output_aliases=aliases,
        cost_estimate=pl.CostEstimate(flops=0, bytes_accessed=0, transcendentals=0),
        name="attend",
        **PARAMS,
    )(*inputs, *so_far)


def finish_kernel(down_ref, *rest):
    backs = rest[:2]
    dkey_ref, dvalue_ref = rest[-2:]
    for part, out in enumerate((dkey_ref, dvalue_ref)):
        total = down_ref[part]
        for back in backs:
            total = total + back[part].astype(jnp.float32)
        out[0] = total.astype(out.dtype)


def finish_chunk(first, down, back, width, so_far):
    _, rows, _ = down.shape
    heads = down.shape[2] // HEAD_DIM
    spec = pl.BlockSpec((2, rows, HEAD_DIM), lambda i: (0, 0, i))
    out_spec = pl.BlockSpec((1, rows, HEAD_DIM), lambda i: (0, 0, first + i))
    inputs = [down, *back]
    return pl.pallas_call(
        finish_kernel,
        grid=(heads,),
        in_specs=[spec] * (1 + len(back))
        + [pl.BlockSpec(memory_space=pl.ANY)] * len(so_far),
        out_specs=[out_spec] * 2,
        out_shape=[jax.ShapeDtypeStruct((1, rows, width), jnp.bfloat16)] * 2,
        input_output_aliases={len(inputs) + i: i for i in range(len(so_far))},
        cost_estimate=pl.CostEstimate(flops=0, bytes_accessed=0, transcendentals=0),
        name="finish",
        **PARAMS,
    )(*inputs, *so_far)


def spread(value, axis, groups=None):
    size = len(groups[0]) if groups else lax.axis_size(axis)
    copies = jnp.broadcast_to(value[None], (size, *value.shape))
    return lax.all_to_all(copies, axis, 0, 0, axis_index_groups=groups)


def body(
    resp_queries, resp_keys, resp_values, grad_out, prompt_keys, prompt_values, rewards, lengths
):
    rows = resp_queries.shape[1]
    width = resp_keys.shape[2]
    seq_size = lax.axis_size("seq")
    resp_all = seq_size // RESP_DEVS
    seq_index = lax.axis_index("seq")
    place = seq_index % RESP_DEVS
    response_id = seq_index // RESP_DEVS
    resp_count = lengths.shape[1]
    prompt_part = prompt_keys.shape[1]
    along = [[r * RESP_DEVS + b for b in range(RESP_DEVS)] for r in range(resp_all)]
    across = [[r * RESP_DEVS + b for r in range(resp_all)] for b in range(RESP_DEVS)]

    def moved(value, *pairs):
        pairs = [(line[a], line[b]) for line in along for a, b in pairs]
        return lax.ppermute(value, "seq", pairs)

    own, own_low, own_high = pack(resp_keys, resp_values)
    low = own_low.shape[2]
    one = moved(own, (0, 1), (1, 2), (2, 3))
    low_three = moved(own_low, (0, 3), (1, 0))
    own_high, low_three = lax.optimization_barrier((own_high, low_three))
    low_two = moved(low_three, (0, 3), (3, 2))
    high_three = moved(own_high, (0, 3))
    high_two = moved(one[:, :, low:], (1, 2), (2, 3))

    prompt_own = jnp.concatenate([prompt_keys[0], prompt_values[0]], axis=1)
    prompt = spread(prompt_own, "seq", along).reshape(RESP_DEVS * prompt_part, 2 * width)
    prompt = spread(prompt, "seq", across).reshape(seq_size * prompt_part, 2 * width)

    group_count = jnp.sum(lengths.astype(jnp.float32)).reshape(1, 1)
    group_count, prompt = lax.optimization_barrier((group_count, prompt))
    count = jnp.sum(spread(group_count, "group"))
    advantage = rewards[0] - jnp.mean(rewards[0])
    advantage = advantage * jnp.float32(lax.axis_size("group") * resp_count * RESP_MAX) / count
    chosen = jnp.arange(resp_count, dtype=jnp.int32) == response_id
    weight = jnp.sum(jnp.where(chosen, advantage, jnp.float32(0.0))).reshape(1)
    length = jnp.sum(jnp.where(chosen, lengths[0], 0))
    where_it_is = jnp.stack([place, length]).astype(jnp.int32)

    fixed = where_it_is, weight, resp_queries, grad_out, prompt, own
    *so_far, down_low, b1, b2, b3 = attend_chunk(
        0, LOW_HEADS, *fixed, (one, low_two, low_three), []
    )
    low_passed = moved(b2, (2, 3), (3, 0))
    low_one = moved(b1, (3, 2), (2, 1), (1, 0))
    low_around = moved(b3 + low_passed, (3, 0), (0, 1))
    *so_far, down_high, b1, b2, b3 = attend_chunk(
        LOW_HEADS, width // HEAD_DIM - LOW_HEADS, *fixed, (one, high_two, high_three), so_far
    )
    high_passed = moved(b2, (3, 2), (2, 1))
    high_around = moved(b3, (3, 0))
    high_one = moved(b1 + high_passed, (3, 2), (2, 1), (1, 0))
    dquery, *dprompt = so_far
    terms = jnp.concatenate(dprompt, axis=1).reshape(resp_all, -1, 2 * width)
    terms, *_ = lax.optimization_barrier(
        (terms, low_one, low_passed, high_passed, high_around)
    )

    done = finish_chunk(0, down_low, (low_one, low_around), width, [])
    done = finish_chunk(LOW_HEADS, down_high, (high_one, high_around), width, done)

    got = lax.all_to_all(terms, "seq", 0, 0, axis_index_groups=across)
    line_sum = jnp.sum(got.astype(jnp.float32), axis=0)
    sent = line_sum.astype(jnp.bfloat16).reshape(RESP_DEVS, prompt_part, 2 * width)
    got = lax.all_to_all(sent, "seq", 0, 0, axis_index_groups=along)
    prompt_sum = jnp.sum(got.astype(jnp.float32), axis=0).astype(jnp.bfloat16)
    return (
        dquery,
        done[0],
        done[1],
        prompt_sum[None, :, :width],
        prompt_sum[None, :, width:],
    )


def solution(mesh):
    split = P("group", "seq", None)
    return jax.shard_map(
        body,
        mesh=mesh,
        in_specs=(split,) * 6 + (P("group", None),) * 2,
        out_specs=(split,) * 5,
        check_vma=False,
    )
```

```python
import jax
import jax.numpy as jnp
from jax import lax
from jax.experimental import pallas as pl
from jax.experimental.pallas import tpu as pltpu
from jax.sharding import PartitionSpec as P

HEAD_DIM = 128
RESP_DEVS = 4
RESP_MAX = 512
LOW_HEADS = 4

SCORE_SCALE = 144.0 ** (-0.5)
LOGIT_CAP = 50.0
VMEM_BYTES = 48 * 1024 * 1024
PARAMS = dict(compiler_params=pltpu.CompilerParams(vmem_limit_bytes=VMEM_BYTES))


def contract(left, right, left_dim, right_dim):
    return lax.dot_general(
        left, right, (((left_dim,), (right_dim,)), ((), ())), preferred_element_type=jnp.float32
    )


def pack_kernel(key_ref, value_ref, all_ref, low_ref, high_ref):
    low = low_ref.shape[2]
    for part, ref in enumerate((key_ref, value_ref)):
        all_ref[part] = ref[0]
        low_ref[part] = ref[0, :, :low]
        high_ref[part] = ref[0, :, low:]


def pack(keys, values):
    _, rows, width = keys.shape
    low = LOW_HEADS * HEAD_DIM
    return pl.pallas_call(
        pack_kernel,
        out_shape=[
            jax.ShapeDtypeStruct((2, rows, wide), keys.dtype) for wide in (width, low, width - low)
        ],
        name="pack",
        **PARAMS,
    )(keys, values)


def attend_kernel(place_ref, weight_ref, query_ref, grad_ref, prompt_key_ref, prompt_value_ref, own_ref, *rest):
    fars = rest[: RESP_DEVS - 1]
    dquery_ref, dprompt_key_ref, dprompt_value_ref, down_ref, *dfars = rest[-(RESP_DEVS + 3) :]
    rows = query_ref.shape[1]
    pair = query_ref.shape[2] // HEAD_DIM
    place, length = place_ref[0], place_ref[1]
    slot = place * rows + lax.broadcasted_iota(jnp.int32, (rows, 1), 0)
    row_weight = jnp.where(slot < length, weight_ref[0], jnp.float32(0.0))
    blocks = [own_ref, *fars]
    prompt_rows = prompt_key_ref.shape[0]
    total_keys = prompt_rows + RESP_DEVS * rows
    key_index = lax.broadcasted_iota(jnp.int32, (pair * rows, total_keys), 1)
    row_index = lax.broadcasted_iota(jnp.int32, (pair * rows, total_keys), 0) % rows
    last_far = prompt_rows + rows * (1 + place)
    own_key = key_index - prompt_rows
    visible = (key_index < last_far) & ((own_key >= rows) | (own_key <= row_index))
    keys = jnp.concatenate([prompt_key_ref[...]] + [block[0] for block in blocks], axis=0)
    values = jnp.concatenate([prompt_value_ref[...]] + [block[1] for block in blocks], axis=0)
    cols = [slice(i * HEAD_DIM, (i + 1) * HEAD_DIM) for i in range(pair)]
    queries = jnp.concatenate([query_ref[0, :, c] for c in cols], axis=0)
    grads = jnp.concatenate(
        [(row_weight * grad_ref[0, :, c].astype(jnp.float32)).astype(jnp.bfloat16) for c in cols],
        axis=0,
    )
    squashed = jnp.tanh(contract(queries, keys, 1, 1) * (SCORE_SCALE / LOGIT_CAP))
    exp_score = jnp.where(visible, jnp.exp(LOGIT_CAP * squashed), jnp.float32(0.0))
    attn = exp_score * (1.0 / jnp.sum(exp_score, axis=1, keepdims=True))
    attn_low = attn.astype(jnp.bfloat16)
    output = contract(attn_low, values, 1, 0).astype(jnp.bfloat16)
    delta = jnp.sum(grads.astype(jnp.float32) * output.astype(jnp.float32), axis=1, keepdims=True)
    grad_weight = contract(grads, values, 1, 1)
    grad_score = (
        attn * (grad_weight - delta) * (SCORE_SCALE - SCORE_SCALE * squashed * squashed)
    ).astype(jnp.bfloat16)
    dquery = contract(grad_score, keys, 1, 0).astype(jnp.bfloat16)
    for i, c in enumerate(cols):
        dquery_ref[0, :, c] = dquery[i * rows : (i + 1) * rows]
    dkeys = contract(grad_score, queries, 0, 0)
    dvalues = contract(attn_low, grads, 0, 0)
    dprompt_key_ref[...] = dkeys[:prompt_rows].astype(dprompt_key_ref.dtype)
    dprompt_value_ref[...] = dvalues[:prompt_rows].astype(dprompt_value_ref.dtype)
    start = prompt_rows
    for out in (down_ref, *dfars):
        stop = start + out.shape[1]
        out[0] = dkeys[start:stop].astype(out.dtype)
        out[1] = dvalues[start:stop].astype(out.dtype)
        start = stop


def attend_chunk(first, heads, where_it_is, weight, queries, grads, prompt, own, far, so_far):
    rows = queries.shape[1]
    all_heads = prompt.shape[1] // 2 // HEAD_DIM
    width = heads * HEAD_DIM
    qcols = queries.shape[2] // all_heads
    smem = pl.BlockSpec(memory_space=pltpu.SMEM)
    query_spec = pl.BlockSpec((1, rows, qcols), lambda i: (0, 0, first + i))
    prompt_block = (prompt.shape[0], HEAD_DIM)
    key_spec = pl.BlockSpec(prompt_block, lambda i: (0, first + i))
    value_spec = pl.BlockSpec(prompt_block, lambda i: (0, all_heads + first + i))
    own_spec = pl.BlockSpec((2, rows, HEAD_DIM), lambda i: (0, 0, i))
    held_specs = [
        pl.BlockSpec(
            (2, rows, HEAD_DIM),
            lambda i, base=first if held.shape[2] > width else 0: (0, 0, base + i),
        )
        for held in (own, *far)
    ]
    outs = [
        jax.ShapeDtypeStruct(queries.shape, jnp.bfloat16),
        jax.ShapeDtypeStruct((prompt.shape[0], all_heads * HEAD_DIM), jnp.bfloat16),
        jax.ShapeDtypeStruct((prompt.shape[0], all_heads * HEAD_DIM), jnp.bfloat16),
        jax.ShapeDtypeStruct((2, rows, width), jnp.float32),
    ] + [jax.ShapeDtypeStruct((2, rows, width), jnp.bfloat16) for _ in far]
    inputs = [where_it_is, weight, queries, grads, prompt, prompt, own, *far]
    specs = [smem, smem, query_spec, query_spec, key_spec, value_spec] + held_specs
    aliases = {len(inputs) + i: i for i in range(len(so_far))}
    return pl.pallas_call(
        attend_kernel,
        grid=(heads,),
        in_specs=specs + [pl.BlockSpec(memory_space=pl.ANY)] * len(so_far),
        out_specs=[query_spec, key_spec, key_spec] + [own_spec] * RESP_DEVS,
        out_shape=outs,
        input_output_aliases=aliases,
        cost_estimate=pl.CostEstimate(flops=0, bytes_accessed=0, transcendentals=0),
        name="attend",
        **PARAMS,
    )(*inputs, *so_far)


def finish_kernel(scale_ref, down_ref, *rest):
    backs = rest[:2]
    dkey_ref, dvalue_ref = rest[-2:]
    for part, out in enumerate((dkey_ref, dvalue_ref)):
        total = down_ref[part]
        for back in backs:
            total = total + back[part].astype(jnp.float32)
        out[0] = (scale_ref[0] * total).astype(out.dtype)


def finish_chunk(first, scale, down, back, width, so_far):
    _, rows, _ = down.shape
    heads = down.shape[2] // HEAD_DIM
    spec = pl.BlockSpec((2, rows, HEAD_DIM), lambda i: (0, 0, i))
    out_spec = pl.BlockSpec((1, rows, HEAD_DIM), lambda i: (0, 0, first + i))
    inputs = [scale, down, *back]
    return pl.pallas_call(
        finish_kernel,
        grid=(heads,),
        in_specs=[pl.BlockSpec(memory_space=pltpu.SMEM)]
        + [spec] * (1 + len(back))
        + [pl.BlockSpec(memory_space=pl.ANY)] * len(so_far),
        out_specs=[out_spec] * 2,
        out_shape=[jax.ShapeDtypeStruct((1, rows, width), jnp.bfloat16)] * 2,
        input_output_aliases={len(inputs) + i: i for i in range(len(so_far))},
        cost_estimate=pl.CostEstimate(flops=0, bytes_accessed=0, transcendentals=0),
        name="finish",
        **PARAMS,
    )(*inputs, *so_far)


def spread(value, axis, groups=None):
    size = len(groups[0]) if groups else lax.axis_size(axis)
    copies = jnp.broadcast_to(value[None], (size, *value.shape))
    return lax.all_to_all(copies, axis, 0, 0, axis_index_groups=groups)


def body(
    resp_queries, resp_keys, resp_values, grad_out, prompt_keys, prompt_values, rewards, lengths
):
    rows = resp_queries.shape[1]
    width = resp_keys.shape[2]
    seq_size = lax.axis_size("seq")
    resp_all = seq_size // RESP_DEVS
    seq_index = lax.axis_index("seq")
    place = seq_index % RESP_DEVS
    response_id = seq_index // RESP_DEVS
    resp_count = lengths.shape[1]
    prompt_part = prompt_keys.shape[1]
    along = [[r * RESP_DEVS + b for b in range(RESP_DEVS)] for r in range(resp_all)]
    across = [[r * RESP_DEVS + b for r in range(resp_all)] for b in range(RESP_DEVS)]

    def moved(value, *pairs):
        pairs = [(line[a], line[b]) for line in along for a, b in pairs]
        return lax.ppermute(value, "seq", pairs)

    own, own_low, own_high = pack(resp_keys, resp_values)
    low = own_low.shape[2]
    one = moved(own, (0, 1), (1, 2), (2, 3))
    low_three = moved(own_low, (0, 3), (1, 0))
    own_high, one = lax.optimization_barrier((own_high, one))
    low_two = moved(low_three, (0, 3), (3, 2))
    high_three = moved(own_high, (0, 3))
    high_two = moved(one[:, :, low:], (1, 2), (2, 3))

    prompt_own = jnp.concatenate([prompt_keys[0], prompt_values[0]], axis=1)
    prompt_own, own = lax.optimization_barrier((prompt_own, own))
    turns = [[(b, (b + d) % RESP_DEVS) for b in range(RESP_DEVS)] for d in (1, 2, 3)]
    prompt = jnp.concatenate([prompt_own] + [moved(prompt_own, *turn) for turn in turns], axis=0)
    prompt, low_three = lax.optimization_barrier((prompt, low_three))
    prompt = spread(prompt, "seq", across).reshape(seq_size * prompt_part, 2 * width)

    advantage = rewards[0] - jnp.mean(rewards[0])
    chosen = jnp.arange(resp_count, dtype=jnp.int32) == response_id
    weight = jnp.sum(jnp.where(chosen, advantage, jnp.float32(0.0))).reshape(1)
    length = jnp.sum(jnp.where(chosen, lengths[0], 0))
    where_it_is = jnp.stack([place, length]).astype(jnp.int32)

    fixed = where_it_is, weight, resp_queries, grad_out, prompt, own
    *so_far, down_low, b1, b2, b3 = attend_chunk(
        0, LOW_HEADS, *fixed, (one, low_two, low_three), []
    )
    low_passed = moved(b2, (2, 3), (3, 0))
    low_one = moved(b1, (3, 2), (2, 1), (1, 0))
    low_around = moved(b3 + low_passed, (3, 0), (0, 1))
    *so_far, down_high, b1, b2, b3 = attend_chunk(
        LOW_HEADS, width // HEAD_DIM - LOW_HEADS, *fixed, (one, high_two, high_three), so_far
    )
    high_passed = moved(b2, (3, 2), (2, 1))
    high_around = moved(b3, (3, 0))
    high_one = moved(b1 + high_passed, (3, 2), (2, 1), (1, 0))
    dquery, *dprompt = so_far
    terms = jnp.concatenate(dprompt, axis=1).reshape(resp_all, -1, 2 * width)
    terms, *_ = lax.optimization_barrier(
        (terms, low_one, low_passed, high_passed, high_around)
    )

    group_count = jnp.sum(lengths.astype(jnp.float32)).reshape(1, 1)
    group_count, low_passed = lax.optimization_barrier((group_count, low_passed))
    count = jnp.sum(spread(group_count, "group"))
    scale = (jnp.float32(lax.axis_size("group") * resp_count * RESP_MAX) / count).reshape(1)

    done = finish_chunk(0, scale, down_low, (low_one, low_around), width, [])
    done = finish_chunk(LOW_HEADS, scale, down_high, (high_one, high_around), width, done)

    got = lax.all_to_all(terms, "seq", 0, 0, axis_index_groups=across)
    line_sum = jnp.sum(got.astype(jnp.float32), axis=0)
    line_sum = line_sum.astype(jnp.bfloat16).reshape(RESP_DEVS, prompt_part, 2 * width)
    sent = jnp.stack(
        [
            sum(
                jnp.where((place - b) % RESP_DEVS == d, line_sum[d], jnp.bfloat16(0.0))
                for d in range(RESP_DEVS)
            )
            for b in range(RESP_DEVS)
        ]
    )
    got = lax.all_to_all(sent, "seq", 0, 0, axis_index_groups=along)
    prompt_sum = (scale * jnp.sum(got.astype(jnp.float32), axis=0)).astype(jnp.bfloat16)
    return (
        (scale * dquery.astype(jnp.float32)).astype(jnp.bfloat16),
        done[0],
        done[1],
        prompt_sum[None, :, :width],
        prompt_sum[None, :, width:],
    )


def solution(mesh):
    split = P("group", "seq", None)
    return jax.shard_map(
        body,
        mesh=mesh,
        in_specs=(split,) * 6 + (P("group", None),) * 2,
        out_specs=(split,) * 5,
        check_vma=False,
    )
```

```python
import jax
import jax.numpy as jnp
from jax import lax
from jax.experimental import pallas as pl
from jax.experimental.pallas import tpu as pltpu
from jax.sharding import PartitionSpec as P

HEAD_DIM = 128
RESP_DEVS = 4
RESP_MAX = 512
LOW_HEADS = 4

SCORE_SCALE = 144.0 ** (-0.5)
LOGIT_CAP = 50.0
COUNT_BASE = 128.0
VMEM_BYTES = 48 * 1024 * 1024
PARAMS = dict(compiler_params=pltpu.CompilerParams(vmem_limit_bytes=VMEM_BYTES))


def contract(left, right, left_dim, right_dim):
    return lax.dot_general(
        left, right, (((left_dim,), (right_dim,)), ((), ())), preferred_element_type=jnp.float32
    )


def pack_kernel(key_ref, value_ref, all_ref, low_ref, high_ref):
    low = low_ref.shape[2]
    for part, ref in enumerate((key_ref, value_ref)):
        all_ref[part] = ref[0]
        low_ref[part] = ref[0, :, :low]
        high_ref[part] = ref[0, :, low:]


def pack(keys, values):
    _, rows, width = keys.shape
    low = LOW_HEADS * HEAD_DIM
    return pl.pallas_call(
        pack_kernel,
        out_shape=[
            jax.ShapeDtypeStruct((2, rows, wide), keys.dtype) for wide in (width, low, width - low)
        ],
        name="pack",
        **PARAMS,
    )(keys, values)


def attend_kernel(place_ref, weight_ref, query_ref, grad_ref, prompt_key_ref, prompt_value_ref, own_ref, *rest):
    fars = rest[: RESP_DEVS - 1]
    dquery_ref, dprompt_ref, down_ref, *dfars = rest[-(RESP_DEVS + 2) :]
    rows = query_ref.shape[1]
    pair = query_ref.shape[2] // HEAD_DIM
    place, length = place_ref[0], place_ref[1]
    slot = place * rows + lax.broadcasted_iota(jnp.int32, (rows, 1), 0)
    row_weight = jnp.where(slot < length, weight_ref[0], jnp.float32(0.0))
    blocks = [own_ref, *fars]
    prompt_rows = prompt_key_ref.shape[0]
    total_keys = prompt_rows + RESP_DEVS * rows
    key_index = lax.broadcasted_iota(jnp.int32, (pair * rows, total_keys), 1)
    row_index = lax.broadcasted_iota(jnp.int32, (pair * rows, total_keys), 0) % rows
    last_far = prompt_rows + rows * (1 + place)
    own_key = key_index - prompt_rows
    visible = (key_index < last_far) & ((own_key >= rows) | (own_key <= row_index))
    keys = jnp.concatenate([prompt_key_ref[...]] + [block[0] for block in blocks], axis=0)
    values = jnp.concatenate([prompt_value_ref[...]] + [block[1] for block in blocks], axis=0)
    cols = [slice(i * HEAD_DIM, (i + 1) * HEAD_DIM) for i in range(pair)]
    queries = jnp.concatenate([query_ref[0, :, c] for c in cols], axis=0)
    grads = jnp.concatenate(
        [(row_weight * grad_ref[0, :, c].astype(jnp.float32)).astype(jnp.bfloat16) for c in cols],
        axis=0,
    )
    squashed = jnp.tanh(contract(queries, keys, 1, 1) * (SCORE_SCALE / LOGIT_CAP))
    exp_score = jnp.where(visible, jnp.exp(LOGIT_CAP * squashed), jnp.float32(0.0))
    attn = exp_score * (1.0 / jnp.sum(exp_score, axis=1, keepdims=True))
    attn_low = attn.astype(jnp.bfloat16)
    output = contract(attn_low, values, 1, 0).astype(jnp.bfloat16)
    delta = jnp.sum(grads.astype(jnp.float32) * output.astype(jnp.float32), axis=1, keepdims=True)
    grad_weight = contract(grads, values, 1, 1)
    grad_score = (
        attn * (grad_weight - delta) * (SCORE_SCALE - SCORE_SCALE * squashed * squashed)
    ).astype(jnp.bfloat16)
    dquery = contract(grad_score, keys, 1, 0).astype(jnp.bfloat16)
    for i, c in enumerate(cols):
        dquery_ref[0, :, c] = dquery[i * rows : (i + 1) * rows]
    dkeys = contract(grad_score, queries, 0, 0)
    dvalues = contract(attn_low, grads, 0, 0)
    wide = dprompt_ref.shape[1] // 2
    for base, part in ((0, dkeys), (wide, dvalues)):
        cols = pl.multiple_of(base + pl.program_id(0) * HEAD_DIM, HEAD_DIM)
        dprompt_ref[:, pl.ds(cols, HEAD_DIM)] = part[:prompt_rows].astype(dprompt_ref.dtype)
    start = prompt_rows
    for out in (down_ref, *dfars):
        stop = start + out.shape[1]
        out[0] = dkeys[start:stop].astype(out.dtype)
        out[1] = dvalues[start:stop].astype(out.dtype)
        start = stop


def attend_chunk(first, heads, where_it_is, weight, queries, grads, prompt, own, far, so_far):
    rows = queries.shape[1]
    all_heads = (prompt.shape[1] - HEAD_DIM) // 2 // HEAD_DIM
    width = heads * HEAD_DIM
    qcols = queries.shape[2] // all_heads
    smem = pl.BlockSpec(memory_space=pltpu.SMEM)
    query_spec = pl.BlockSpec((1, rows, qcols), lambda i: (0, 0, first + i))
    prompt_block = (prompt.shape[0], HEAD_DIM)
    key_spec = pl.BlockSpec(prompt_block, lambda i: (0, first + i))
    value_spec = pl.BlockSpec(prompt_block, lambda i: (0, all_heads + first + i))
    own_spec = pl.BlockSpec((2, rows, HEAD_DIM), lambda i: (0, 0, i))
    held_specs = [
        pl.BlockSpec(
            (2, rows, HEAD_DIM),
            lambda i, base=first if held.shape[2] > width else 0: (0, 0, base + i),
        )
        for held in (own, *far)
    ]
    outs = [
        jax.ShapeDtypeStruct(queries.shape, jnp.bfloat16),
        jax.ShapeDtypeStruct((prompt.shape[0], 2 * width), jnp.bfloat16),
        jax.ShapeDtypeStruct((2, rows, width), jnp.float32),
    ] + [jax.ShapeDtypeStruct((2, rows, width), jnp.bfloat16) for _ in far]
    inputs = [where_it_is, weight, queries, grads, prompt, prompt, own, *far]
    specs = [smem, smem, query_spec, query_spec, key_spec, value_spec] + held_specs
    aliases = {len(inputs) + i: i for i in range(len(so_far))}
    return pl.pallas_call(
        attend_kernel,
        grid=(heads,),
        in_specs=specs + [pl.BlockSpec(memory_space=pl.ANY)] * len(so_far),
        out_specs=[query_spec, pl.BlockSpec(outs[1].shape, lambda i: (0, 0))] + [own_spec] * RESP_DEVS,
        out_shape=outs,
        input_output_aliases=aliases,
        cost_estimate=pl.CostEstimate(flops=0, bytes_accessed=0, transcendentals=0),
        name="attend",
        **PARAMS,
    )(*inputs, *so_far)


def finish_kernel(down_ref, *rest):
    backs = rest[:2]
    dkey_ref, dvalue_ref = rest[-2:]
    for part, out in enumerate((dkey_ref, dvalue_ref)):
        total = down_ref[part]
        for back in backs:
            total = total + back[part].astype(jnp.float32)
        out[0] = total.astype(out.dtype)


def finish_chunk(first, down, back, width, so_far):
    _, rows, _ = down.shape
    heads = down.shape[2] // HEAD_DIM
    spec = pl.BlockSpec((2, rows, HEAD_DIM), lambda i: (0, 0, i))
    out_spec = pl.BlockSpec((1, rows, HEAD_DIM), lambda i: (0, 0, first + i))
    inputs = [down, *back]
    return pl.pallas_call(
        finish_kernel,
        grid=(heads,),
        in_specs=[spec] * (1 + len(back))
        + [pl.BlockSpec(memory_space=pl.ANY)] * len(so_far),
        out_specs=[out_spec] * 2,
        out_shape=[jax.ShapeDtypeStruct((1, rows, width), jnp.bfloat16)] * 2,
        input_output_aliases={len(inputs) + i: i for i in range(len(so_far))},
        cost_estimate=pl.CostEstimate(flops=0, bytes_accessed=0, transcendentals=0),
        name="finish",
        **PARAMS,
    )(*inputs, *so_far)


def spread(value, axis, groups=None):
    size = len(groups[0]) if groups else lax.axis_size(axis)
    copies = jnp.broadcast_to(value[None], (size, *value.shape))
    return lax.all_to_all(copies, axis, 0, 0, axis_index_groups=groups)


def body(
    resp_queries, resp_keys, resp_values, grad_out, prompt_keys, prompt_values, rewards, lengths
):
    rows = resp_queries.shape[1]
    width = resp_keys.shape[2]
    seq_size = lax.axis_size("seq")
    resp_all = seq_size // RESP_DEVS
    seq_index = lax.axis_index("seq")
    place = seq_index % RESP_DEVS
    response_id = seq_index // RESP_DEVS
    resp_count = lengths.shape[1]
    prompt_part = prompt_keys.shape[1]
    along = [[r * RESP_DEVS + b for b in range(RESP_DEVS)] for r in range(resp_all)]
    across = [[r * RESP_DEVS + b for r in range(resp_all)] for b in range(RESP_DEVS)]

    def moved(value, *pairs):
        pairs = [(line[a], line[b]) for line in along for a, b in pairs]
        return lax.ppermute(value, "seq", pairs)

    own, own_low, own_high = pack(resp_keys, resp_values)
    low = own_low.shape[2]
    one = moved(own, (0, 1), (1, 2), (2, 3))
    low_three = moved(own_low, (0, 3), (1, 0))
    own_high, one = lax.optimization_barrier((own_high, one))
    low_two = moved(low_three, (0, 3), (3, 2))
    high_three = moved(own_high, (0, 3))
    high_two = moved(one[:, :, low:], (1, 2), (2, 3))

    groups = lax.axis_size("group")
    own_count = jnp.sum(lengths.astype(jnp.float32)).reshape(1, 1)
    pairs = [
        (g * seq_size + s, (g + s // RESP_DEVS) % groups * seq_size + s)
        for g in range(groups)
        for s in range(seq_size)
        if s // RESP_DEVS % groups
    ]
    other_count = lax.ppermute(own_count, ("group", "seq"), pairs)
    other_count = jnp.where(response_id % groups == 0, own_count, other_count)

    prompt_own = jnp.concatenate([prompt_keys[0], prompt_values[0]], axis=1)
    prompt_own, other_count, own = lax.optimization_barrier((prompt_own, other_count, own))
    turns = [[(b, (b + d) % RESP_DEVS) for b in range(RESP_DEVS)] for d in (1, 2, 3)]
    prompt = jnp.concatenate([prompt_own] + [moved(prompt_own, *turn) for turn in turns], axis=0)
    prompt, low_three = lax.optimization_barrier((prompt, low_three))
    cell = jnp.arange(HEAD_DIM)[None, :]
    high = jnp.floor(other_count / COUNT_BASE)
    cells = jnp.where(cell == 0, high, jnp.where(cell == 1, other_count - high * COUNT_BASE, 0.0))
    cells = jnp.broadcast_to(cells.astype(jnp.bfloat16), (prompt.shape[0], HEAD_DIM))
    prompt = spread(jnp.concatenate([prompt, cells], axis=1), "seq", across)
    parts = prompt[:, 0, 2 * width : 2 * width + 2].astype(jnp.float32)
    prompt = prompt.reshape(seq_size * prompt_part, 2 * width + HEAD_DIM)

    count = jnp.sum(parts[:, 0] * COUNT_BASE + parts[:, 1]) * (groups / resp_all)
    advantage = rewards[0] - jnp.mean(rewards[0])
    advantage = advantage * jnp.float32(lax.axis_size("group") * resp_count * RESP_MAX) / count
    chosen = jnp.arange(resp_count, dtype=jnp.int32) == response_id
    weight = jnp.sum(jnp.where(chosen, advantage, jnp.float32(0.0))).reshape(1)
    length = jnp.sum(jnp.where(chosen, lengths[0], 0))
    where_it_is = jnp.stack([place, length]).astype(jnp.int32)

    fixed = where_it_is, weight, resp_queries, grad_out, prompt, own
    dquery, terms_low, down_low, b1, b2, b3 = attend_chunk(
        0, LOW_HEADS, *fixed, (one, low_two, low_three), []
    )
    low_passed = moved(b2, (2, 3), (3, 0))
    low_one = moved(b1, (3, 2), (2, 1), (1, 0))
    low_around = moved(b3 + low_passed, (3, 0), (0, 1))
    dquery, terms_high, down_high, b1, b2, b3 = attend_chunk(
        LOW_HEADS, width // HEAD_DIM - LOW_HEADS, *fixed, (one, high_two, high_three), [dquery]
    )
    high_passed = moved(b2, (3, 2), (2, 1))
    high_around = moved(b3, (3, 0))
    high_one = moved(b1 + high_passed, (3, 2), (2, 1), (1, 0))
    low = LOW_HEADS * HEAD_DIM
    terms_low, terms_high = [
        terms.reshape(resp_all, -1, terms.shape[1]) for terms in (terms_low, terms_high)
    ]
    terms_low, *_ = lax.optimization_barrier((terms_low, low_one, low_passed))

    done = finish_chunk(0, down_low, (low_one, low_around), width, [])
    done = finish_chunk(LOW_HEADS, down_high, (high_one, high_around), width, done)

    line_low, line_high = [
        jnp.sum(
            lax.all_to_all(terms, "seq", 0, 0, axis_index_groups=across).astype(jnp.float32), axis=0
        ).astype(jnp.bfloat16)
        for terms in (terms_low, terms_high)
    ]
    line_low, *_ = lax.optimization_barrier((line_low, high_passed, high_around))
    line_sum = jnp.concatenate(
        [line_low[:, :low], line_high[:, : width - low], line_low[:, low:], line_high[:, width - low :]],
        axis=1,
    )
    line_sum = line_sum.reshape(RESP_DEVS, prompt_part, 2 * width)
    sent = jnp.stack(
        [
            sum(
                jnp.where((place - b) % RESP_DEVS == d, line_sum[d], jnp.bfloat16(0.0))
                for d in range(RESP_DEVS)
            )
            for b in range(RESP_DEVS)
        ]
    )
    got = lax.all_to_all(sent, "seq", 0, 0, axis_index_groups=along)
    prompt_sum = jnp.sum(got.astype(jnp.float32), axis=0).astype(jnp.bfloat16)
    return (
        dquery,
        done[0],
        done[1],
        prompt_sum[None, :, :width],
        prompt_sum[None, :, width:],
    )


def solution(mesh):
    split = P("group", "seq", None)
    return jax.shard_map(
        body,
        mesh=mesh,
        in_specs=(split,) * 6 + (P("group", None),) * 2,
        out_specs=(split,) * 5,
        check_vma=False,
    )
```

```python
import jax
import jax.numpy as jnp
from jax import lax
from jax.experimental import pallas as pl
from jax.experimental.pallas import tpu as pltpu
from jax.sharding import PartitionSpec as P

HEAD_DIM = 128
RESP_DEVS = 4
RESP_MAX = 512
LOW_HEADS = 4

SCORE_SCALE = 144.0 ** (-0.5)
LOGIT_CAP = 50.0
COUNT_BASE = 128.0
VMEM_BYTES = 48 * 1024 * 1024
PARAMS = dict(compiler_params=pltpu.CompilerParams(vmem_limit_bytes=VMEM_BYTES))


def contract(left, right, left_dim, right_dim):
    return lax.dot_general(
        left, right, (((left_dim,), (right_dim,)), ((), ())), preferred_element_type=jnp.float32
    )


def pack_kernel(key_ref, value_ref, all_ref, low_ref, high_ref):
    low = low_ref.shape[2]
    for part, ref in enumerate((key_ref, value_ref)):
        all_ref[part] = ref[0]
        low_ref[part] = ref[0, :, :low]
        high_ref[part] = ref[0, :, low:]


def pack(keys, values):
    _, rows, width = keys.shape
    low = LOW_HEADS * HEAD_DIM
    return pl.pallas_call(
        pack_kernel,
        out_shape=[
            jax.ShapeDtypeStruct((2, rows, wide), keys.dtype) for wide in (width, low, width - low)
        ],
        name="pack",
        **PARAMS,
    )(keys, values)


def attend_kernel(place_ref, weight_ref, query_ref, grad_ref, prompt_key_ref, prompt_value_ref, own_ref, *rest):
    fars = rest[: RESP_DEVS - 1]
    dquery_ref, dprompt_key_ref, dprompt_value_ref, down_ref, *dfars = rest[-(RESP_DEVS + 3) :]
    rows = query_ref.shape[1]
    pair = query_ref.shape[2] // HEAD_DIM
    place, length = place_ref[0], place_ref[1]
    slot = place * rows + lax.broadcasted_iota(jnp.int32, (rows, 1), 0)
    row_weight = jnp.where(slot < length, weight_ref[0], jnp.float32(0.0))
    blocks = [own_ref, *fars]
    prompt_rows = prompt_key_ref.shape[0]
    total_keys = prompt_rows + RESP_DEVS * rows
    key_index = lax.broadcasted_iota(jnp.int32, (pair * rows, total_keys), 1)
    row_index = lax.broadcasted_iota(jnp.int32, (pair * rows, total_keys), 0) % rows
    last_far = prompt_rows + rows * (1 + place)
    own_key = key_index - prompt_rows
    visible = (key_index < last_far) & ((own_key >= rows) | (own_key <= row_index))
    keys = jnp.concatenate([prompt_key_ref[...]] + [block[0] for block in blocks], axis=0)
    values = jnp.concatenate([prompt_value_ref[...]] + [block[1] for block in blocks], axis=0)
    cols = [slice(i * HEAD_DIM, (i + 1) * HEAD_DIM) for i in range(pair)]
    queries = jnp.concatenate([query_ref[0, :, c] for c in cols], axis=0)
    grads = jnp.concatenate(
        [(row_weight * grad_ref[0, :, c].astype(jnp.float32)).astype(jnp.bfloat16) for c in cols],
        axis=0,
    )
    squashed = jnp.tanh(contract(queries, keys, 1, 1) * (SCORE_SCALE / LOGIT_CAP))
    exp_score = jnp.where(visible, jnp.exp(LOGIT_CAP * squashed), jnp.float32(0.0))
    attn = exp_score * (1.0 / jnp.sum(exp_score, axis=1, keepdims=True))
    attn_low = attn.astype(jnp.bfloat16)
    output = contract(attn_low, values, 1, 0).astype(jnp.bfloat16)
    delta = jnp.sum(grads.astype(jnp.float32) * output.astype(jnp.float32), axis=1, keepdims=True)
    grad_weight = contract(grads, values, 1, 1)
    grad_score = (
        attn * (grad_weight - delta) * (SCORE_SCALE - SCORE_SCALE * squashed * squashed)
    ).astype(jnp.bfloat16)
    dquery = contract(grad_score, keys, 1, 0).astype(jnp.bfloat16)
    for i, c in enumerate(cols):
        dquery_ref[0, :, c] = dquery[i * rows : (i + 1) * rows]
    dkeys = contract(grad_score, queries, 0, 0)
    dvalues = contract(attn_low, grads, 0, 0)
    dprompt_key_ref[...] = dkeys[:prompt_rows].astype(dprompt_key_ref.dtype)
    dprompt_value_ref[...] = dvalues[:prompt_rows].astype(dprompt_value_ref.dtype)
    start = prompt_rows
    for out in (down_ref, *dfars):
        stop = start + out.shape[1]
        out[0] = dkeys[start:stop].astype(out.dtype)
        out[1] = dvalues[start:stop].astype(out.dtype)
        start = stop


def attend_chunk(first, heads, where_it_is, weight, queries, grads, prompt, own, far, so_far):
    rows = queries.shape[1]
    all_heads = (prompt.shape[1] - HEAD_DIM) // 2 // HEAD_DIM
    width = heads * HEAD_DIM
    qcols = queries.shape[2] // all_heads
    smem = pl.BlockSpec(memory_space=pltpu.SMEM)
    query_spec = pl.BlockSpec((1, rows, qcols), lambda i: (0, 0, first + i))
    prompt_block = (prompt.shape[0], HEAD_DIM)
    key_spec = pl.BlockSpec(prompt_block, lambda i: (0, first + i))
    value_spec = pl.BlockSpec(prompt_block, lambda i: (0, all_heads + first + i))
    own_spec = pl.BlockSpec((2, rows, HEAD_DIM), lambda i: (0, 0, i))
    held_specs = [
        pl.BlockSpec(
            (2, rows, HEAD_DIM),
            lambda i, base=first if held.shape[2] > width else 0: (0, 0, base + i),
        )
        for held in (own, *far)
    ]
    outs = [
        jax.ShapeDtypeStruct(queries.shape, jnp.bfloat16),
        jax.ShapeDtypeStruct((prompt.shape[0], all_heads * HEAD_DIM), jnp.bfloat16),
        jax.ShapeDtypeStruct((prompt.shape[0], all_heads * HEAD_DIM), jnp.bfloat16),
        jax.ShapeDtypeStruct((2, rows, width), jnp.float32),
    ] + [jax.ShapeDtypeStruct((2, rows, width), jnp.bfloat16) for _ in far]
    inputs = [where_it_is, weight, queries, grads, prompt, prompt, own, *far]
    specs = [smem, smem, query_spec, query_spec, key_spec, value_spec] + held_specs
    aliases = {len(inputs) + i: i for i in range(len(so_far))}
    return pl.pallas_call(
        attend_kernel,
        grid=(heads,),
        in_specs=specs + [pl.BlockSpec(memory_space=pl.ANY)] * len(so_far),
        out_specs=[query_spec, key_spec, key_spec] + [own_spec] * RESP_DEVS,
        out_shape=outs,
        input_output_aliases=aliases,
        cost_estimate=pl.CostEstimate(flops=0, bytes_accessed=0, transcendentals=0),
        name="attend",
        **PARAMS,
    )(*inputs, *so_far)


def finish_kernel(down_ref, *rest):
    backs = rest[:2]
    dkey_ref, dvalue_ref = rest[-2:]
    for part, out in enumerate((dkey_ref, dvalue_ref)):
        total = down_ref[part]
        for back in backs:
            total = total + back[part].astype(jnp.float32)
        out[0] = total.astype(out.dtype)


def finish_chunk(first, down, back, width, so_far):
    _, rows, _ = down.shape
    heads = down.shape[2] // HEAD_DIM
    spec = pl.BlockSpec((2, rows, HEAD_DIM), lambda i: (0, 0, i))
    out_spec = pl.BlockSpec((1, rows, HEAD_DIM), lambda i: (0, 0, first + i))
    inputs = [down, *back]
    return pl.pallas_call(
        finish_kernel,
        grid=(heads,),
        in_specs=[spec] * (1 + len(back))
        + [pl.BlockSpec(memory_space=pl.ANY)] * len(so_far),
        out_specs=[out_spec] * 2,
        out_shape=[jax.ShapeDtypeStruct((1, rows, width), jnp.bfloat16)] * 2,
        input_output_aliases={len(inputs) + i: i for i in range(len(so_far))},
        cost_estimate=pl.CostEstimate(flops=0, bytes_accessed=0, transcendentals=0),
        name="finish",
        **PARAMS,
    )(*inputs, *so_far)


def spread(value, axis, groups=None):
    size = len(groups[0]) if groups else lax.axis_size(axis)
    copies = jnp.broadcast_to(value[None], (size, *value.shape))
    return lax.all_to_all(copies, axis, 0, 0, axis_index_groups=groups)


def body(
    resp_queries, resp_keys, resp_values, grad_out, prompt_keys, prompt_values, rewards, lengths
):
    rows = resp_queries.shape[1]
    width = resp_keys.shape[2]
    seq_size = lax.axis_size("seq")
    resp_all = seq_size // RESP_DEVS
    seq_index = lax.axis_index("seq")
    place = seq_index % RESP_DEVS
    response_id = seq_index // RESP_DEVS
    resp_count = lengths.shape[1]
    prompt_part = prompt_keys.shape[1]
    along = [[r * RESP_DEVS + b for b in range(RESP_DEVS)] for r in range(resp_all)]
    across = [[r * RESP_DEVS + b for r in range(resp_all)] for b in range(RESP_DEVS)]

    def moved(value, *pairs):
        pairs = [(line[a], line[b]) for line in along for a, b in pairs]
        return lax.ppermute(value, "seq", pairs)

    own, own_low, own_high = pack(resp_keys, resp_values)
    low = own_low.shape[2]
    one = moved(own, (0, 1), (1, 2), (2, 3))
    low_three = moved(own_low, (0, 3), (1, 0))
    own_high, one = lax.optimization_barrier((own_high, one))
    low_two = moved(low_three, (0, 3), (3, 2))
    high_three = moved(own_high, (0, 3))
    high_two = moved(one[:, :, low:], (1, 2), (2, 3))

    groups = lax.axis_size("group")
    own_count = jnp.sum(lengths.astype(jnp.float32)).reshape(1, 1)
    pairs = [
        (g * seq_size + s, (g + s // RESP_DEVS) % groups * seq_size + s)
        for g in range(groups)
        for s in range(seq_size)
        if s // RESP_DEVS % groups
    ]
    other_count = lax.ppermute(own_count, ("group", "seq"), pairs)
    other_count = jnp.where(response_id % groups == 0, own_count, other_count)

    prompt_own = jnp.concatenate([prompt_keys[0], prompt_values[0]], axis=1)
    prompt_own, other_count, own = lax.optimization_barrier((prompt_own, other_count, own))
    turns = [[(b, (b + d) % RESP_DEVS) for b in range(RESP_DEVS)] for d in (1, 2, 3)]
    prompt = jnp.concatenate([prompt_own] + [moved(prompt_own, *turn) for turn in turns], axis=0)
    prompt, low_three = lax.optimization_barrier((prompt, low_three))
    cell = jnp.arange(HEAD_DIM)[None, :]
    high = jnp.floor(other_count / COUNT_BASE)
    cells = jnp.where(cell == 0, high, jnp.where(cell == 1, other_count - high * COUNT_BASE, 0.0))
    cells = jnp.broadcast_to(cells.astype(jnp.bfloat16), (prompt.shape[0], HEAD_DIM))
    prompt = spread(jnp.concatenate([prompt, cells], axis=1), "seq", across)
    parts = prompt[:, 0, 2 * width : 2 * width + 2].astype(jnp.float32)
    prompt = prompt.reshape(seq_size * prompt_part, 2 * width + HEAD_DIM)

    count = jnp.sum(parts[:, 0] * COUNT_BASE + parts[:, 1]) * (groups / resp_all)
    advantage = rewards[0] - jnp.mean(rewards[0])
    advantage = advantage * jnp.float32(lax.axis_size("group") * resp_count * RESP_MAX) / count
    chosen = jnp.arange(resp_count, dtype=jnp.int32) == response_id
    weight = jnp.sum(jnp.where(chosen, advantage, jnp.float32(0.0))).reshape(1)
    length = jnp.sum(jnp.where(chosen, lengths[0], 0))
    where_it_is = jnp.stack([place, length]).astype(jnp.int32)

    fixed = where_it_is, weight, resp_queries, grad_out, prompt, own
    *so_far, down_low, b1, b2, b3 = attend_chunk(
        0, LOW_HEADS, *fixed, (one, low_two, low_three), []
    )
    low_passed = moved(b2, (2, 3), (3, 0))
    low_one = moved(b1, (3, 2), (2, 1), (1, 0))
    low_around = moved(b3 + low_passed, (3, 0), (0, 1))
    *so_far, down_high, b1, b2, b3 = attend_chunk(
        LOW_HEADS, width // HEAD_DIM - LOW_HEADS, *fixed, (one, high_two, high_three), so_far
    )
    high_passed = moved(b2, (3, 2), (2, 1))
    high_around = moved(b3, (3, 0))
    high_one = moved(b1 + high_passed, (3, 2), (2, 1), (1, 0))
    dquery, *dprompt = so_far
    terms = jnp.concatenate(dprompt, axis=1).reshape(resp_all, -1, 2 * width)
    terms, *_ = lax.optimization_barrier(
        (terms, low_one, low_passed, high_passed, high_around)
    )

    done = finish_chunk(0, down_low, (low_one, low_around), width, [])
    done = finish_chunk(LOW_HEADS, down_high, (high_one, high_around), width, done)

    got = lax.all_to_all(terms, "seq", 0, 0, axis_index_groups=across)
    line_sum = jnp.sum(got.astype(jnp.float32), axis=0)
    line_sum = line_sum.astype(jnp.bfloat16).reshape(RESP_DEVS, prompt_part, 2 * width)
    parts_back = [
        moved(line_sum[d], *[(b, (b - d) % RESP_DEVS) for b in range(RESP_DEVS)])
        for d in range(1, RESP_DEVS)
    ]
    prompt_sum = sum(p.astype(jnp.float32) for p in [line_sum[0], *parts_back])
    prompt_sum = prompt_sum.astype(jnp.bfloat16)
    return (
        dquery,
        done[0],
        done[1],
        prompt_sum[None, :, :width],
        prompt_sum[None, :, width:],
    )


def solution(mesh):
    split = P("group", "seq", None)
    return jax.shard_map(
        body,
        mesh=mesh,
        in_specs=(split,) * 6 + (P("group", None),) * 2,
        out_specs=(split,) * 5,
        check_vma=False,
    )
```
